32 devices in a mesh: dp: 4 (over z), shard: 8 (over y, x, core).
Axes of the slice: x: 2, y: 2, z: 4, core: 2. Of those that a mesh axis runs over, the one named last changes fastest.
Arguments:
- tokens: bfloat16 [1024, 4096], P(('dp', 'shard')), may hold values from -6 to 6
- cotangent: bfloat16 [1024, 4096], P(('dp', 'shard')), may hold values from -6 to 6
- w_up: bfloat16 [4096, 14336], P('shard', 'dp'), may hold values from -0.09375 to 0.09375
- w_down: bfloat16 [14336, 4096], P('dp', 'shard'), may hold values from -0.046875 to 0.046875
- delta: float32 [128, 128, 128], P(('dp', 'shard')), may hold values from -0.5 to 0.5
- first_moment: float32 [128, 128, 128], P(('dp', 'shard')), may hold values from -1.8 to 1.8
- second_moment: float32 [128, 128, 128], P(('dp', 'shard')), may hold values from 0.02 to 0.3
- blk_row: int32 [128], replicated, may hold values from 0 to 31
- blk_col: int32 [128], replicated, may hold values from 0 to 111, as said below
- live: int32 [128], replicated, may hold values from 0 to 1, as said below
Outputs:
- layer_out: bfloat16 [1024, 4096], P(('dp', 'shard'))
- new_delta: float32 [128, 128, 128], P(('dp', 'shard'))
- new_first: float32 [128, 128, 128], P(('dp', 'shard'))
- new_second: float32 [128, 128, 128], P(('dp', 'shard'))
The draws below stay inside these ranges and needn't reach their ends.
Inputs may be any that keep to these rules, and one draw needn't show every extreme that they name: `blk_col`: slots j to j + 8 * 4 - 1 with j a multiple of 32 name distinct blocks, all with block columns from (j // 32) * 28 to that plus 28 - 1. The live slots of each device come first among its 4 slots; some device has all 4 live.
All inputs are finite; a program needn't handle non-finite values.
Results may differ from the reference program's by a relative error of at most 0.014.
Values may be sent and summed in bfloat16 or wider, within the bound.
A program may use at most 192 MiB of HBM per device.

```python
import math
import jax
import jax.numpy as jnp
from jax import lax

D = 4096
FF = 14336
BLK = 128
OWN = 4
BLOCK_ROWS = 32
BLOCK_COLS = 28
SLOTS = 128
TOKENS = 1024
N_DP = 4
N_SHARD = 8
DEVICES = 32


def pick_cells(key):
    base = jax.random.fold_in(key, 7)
    keys = jax.random.split(base, N_DP)
    return jax.vmap(lambda k: jax.random.permutation(k, BLOCK_ROWS * BLOCK_COLS)[:N_SHARD * OWN])(keys)


def draw_blk_row(key, part):
    cells = pick_cells(key)
    return (cells // BLOCK_COLS).reshape(-1).astype(jnp.int32)


def draw_blk_col(key, part):
    cells = pick_cells(key)
    offsets = jnp.arange(N_DP, dtype=jnp.int32)[:, None] * BLOCK_COLS
    return (cells % BLOCK_COLS + offsets).reshape(-1).astype(jnp.int32)


def draw_live(key, part):
    counts = jax.random.randint(jax.random.fold_in(key, 3), (DEVICES,), 0, OWN + 1)
    chosen = jax.random.randint(jax.random.fold_in(key, 5), (), 0, DEVICES)
    counts = jnp.where(jnp.arange(DEVICES) == chosen, OWN, counts)
    flags = jnp.arange(OWN, dtype=jnp.int32)[None, :] < counts[:, None]
    return flags.reshape(-1).astype(jnp.int32)


def shard_levels(key, shape, shards, low, largest):
    def one(position, parts):
        draws = jax.random.uniform(jax.random.fold_in(jax.random.fold_in(key, 6), position), (parts,), jnp.float32, low / len(shards), largest / len(shards))
        return jnp.repeat(jnp.exp(draws), shape[position] // parts).reshape((-1,) + (1,) * (len(shape) - position - 1))

    loudness = one(*shards[0])
    for cut in shards[1:]:
        loudness = loudness * one(*cut)
    return loudness


def centred(rng, dims, scale, reach, pieces=(), held_as=jnp.bfloat16):
    entries = jax.random.normal(rng, dims, jnp.float32) * scale
    if len(pieces) > 0:
        entries = shard_levels(rng, dims, pieces, -0.22, 0.18) * entries
    return jnp.clip(entries, min=-reach, max=reach).astype(held_as)


def setup_inputs(seed: int = 0) -> dict:
    seeds = jax.random.split(jax.random.key(seed), 11)
    tokens = centred(seeds[0], (TOKENS, D), 1.0, 6.0, ((0, 32),))
    cotangent = centred(seeds[1], (TOKENS, D), 1.0, 6.0, ((0, 32),))
    w_up = centred(seeds[2], (D, FF), D ** -0.5, 0.09375, ((0, 8), (1, 4)))
    w_down = centred(seeds[3], (FF, D), FF ** -0.5, 0.046875, ((0, 4), (1, 8)))
    delta = centred(seeds[4], (SLOTS, BLK, BLK), BLK ** -0.5, 0.5, ((0, 32),), jnp.float32)
    first_moment = centred(seeds[5], (SLOTS, BLK, BLK), 0.3, 1.8, ((0, 32),), jnp.float32)
    second_moment = jnp.clip(jnp.exp(math.log(0.3) - 2.7080503 * jax.random.uniform(seeds[6], (SLOTS, BLK, BLK), jnp.float32) ** shard_levels(seeds[6], (SLOTS, BLK, BLK), ((0, 32),), -0.2, 0.2)), 0.02, 0.3)
    blk_row = draw_blk_row(jax.random.fold_in(seeds[10], 71), 0)
    blk_col = draw_blk_col(jax.random.fold_in(seeds[10], 71), 0)
    live = draw_live(jax.random.fold_in(seeds[10], 71), 0)
    return dict(tokens=tokens, cotangent=cotangent, w_up=w_up, w_down=w_down, delta=delta, first_moment=first_moment, second_moment=second_moment, blk_row=blk_row, blk_col=blk_col, live=live)


def reference(tokens, cotangent, w_up, w_down, delta, first_moment, second_moment, blk_row, blk_col, live):
    blocks = delta.astype(jnp.bfloat16)
    alive = live.astype(jnp.float32)
    pre = jnp.dot(tokens, w_up, preferred_element_type=jnp.float32)

    def add_block(total, item):
        block, row_idx, col_idx, flag = item
        inputs = lax.dynamic_slice_in_dim(tokens, (row_idx * BLK).astype(jnp.int32), BLK, 1)
        term = jnp.dot(inputs, block, preferred_element_type=jnp.float32) * flag
        start = (col_idx * BLK).astype(jnp.int32)
        current = lax.dynamic_slice_in_dim(total, start, BLK, 1)
        return (lax.dynamic_update_slice_in_dim(total, current + term, start, 1), None)
    pre, _ = lax.scan(add_block, pre, (blocks, blk_row, blk_col, alive))
    hidden = jax.nn.silu(pre).astype(jnp.bfloat16)
    layer_out = jnp.dot(hidden, w_down, preferred_element_type=jnp.float32).astype(jnp.bfloat16)
    back = lax.dot_general(cotangent, w_down, (((1,), (1,)), ((), ())), preferred_element_type=jnp.float32)
    sigma = jax.nn.sigmoid(pre)
    dpre = (back * sigma * (1.0 + pre * (1.0 - sigma))).astype(jnp.bfloat16)
    factor = 1.0 / jnp.sqrt(jnp.float32(TOKENS))

    def block_grad(item):
        row_idx, col_idx, flag = item
        inputs = lax.dynamic_slice_in_dim(tokens, (row_idx * BLK).astype(jnp.int32), BLK, 1)
        slope = lax.dynamic_slice_in_dim(dpre, (col_idx * BLK).astype(jnp.int32), BLK, 1)
        prod = lax.dot_general(inputs, slope, (((0,), (0,)), ((), ())), preferred_element_type=jnp.float32)
        return prod * flag * factor
    grads = lax.map(block_grad, (blk_row, blk_col, alive))
    new_first = 0.9 * first_moment + 0.1 * grads
    new_second = 0.95 * second_moment + 0.05 * grads * grads
    corrected_first = new_first / (1.0 - 0.9 ** 10)
    corrected_second = new_second / (1.0 - 0.95 ** 10)
    new_delta = delta - 0.01 * corrected_first / (jnp.sqrt(corrected_second) + 1e-08)
    return (layer_out, new_delta, new_first, new_second)
```

```python
import math

import jax
import jax.numpy as jnp
from jax import lax
from jax.sharding import PartitionSpec as P


def on_device(
    tokens, cotangent, w_up, w_down, delta, first_moment, second_moment, blk_row, blk_col, live
):
    shards = lax.axis_size("shard")
    own_slots = delta.shape[0]
    side = delta.shape[1]
    gathered_x, gathered_d = (
        lax.all_gather(tokens, "dp", axis=0, tiled=True),
        lax.all_gather(cotangent, "dp", axis=0, tiled=True),
    )
    rows = gathered_x.shape[0]
    width = gathered_x.shape[1]
    local_ff = w_up.shape[1]
    col_count = local_ff // side
    row_count = width // side
    group_index = lax.axis_index("dp")
    group_size = shards * own_slots
    begin = group_index * group_size
    slot_row = lax.dynamic_slice_in_dim(blk_row, begin, group_size)
    slot_col = lax.dynamic_slice_in_dim(blk_col, begin, group_size) - group_index * col_count
    slot_live = lax.dynamic_slice_in_dim(live, begin, group_size).astype(jnp.float32)
    row_onehot = (slot_row[:, None] == jnp.arange(row_count)[None, :]).astype(jnp.float32)
    col_onehot = (slot_col[:, None] == jnp.arange(col_count)[None, :]).astype(
        jnp.float32
    ) * slot_live[:, None]
    blocks = lax.all_gather(delta.astype(jnp.bfloat16), "shard", axis=0, tiled=True)
    x_cols = lax.all_to_all(gathered_x, "shard", split_axis=1, concat_axis=0, tiled=True)
    d_cols = lax.all_to_all(gathered_d, "shard", split_axis=1, concat_axis=0, tiled=True)
    pre_part = jnp.dot(x_cols, w_up, preferred_element_type=jnp.float32).astype(jnp.bfloat16)
    pre = lax.psum_scatter(pre_part, "shard", scatter_dimension=0, tiled=True).astype(jnp.float32)
    back_part = lax.dot_general(
        d_cols, w_down, (((1,), (1,)), ((), ())), preferred_element_type=jnp.float32
    ).astype(jnp.bfloat16)
    back = lax.psum_scatter(back_part, "shard", scatter_dimension=0, tiled=True).astype(jnp.float32)
    x_blocks = gathered_x.reshape(rows, row_count, side)
    picked = jnp.einsum(
        "rkb,sk->srb", x_blocks, row_onehot.astype(jnp.bfloat16), preferred_element_type=jnp.float32
    ).astype(jnp.bfloat16)
    contrib = jnp.einsum("srb,sbn->srn", picked, blocks, preferred_element_type=jnp.float32)
    placed = jnp.einsum("srn,sc->rcn", contrib, col_onehot, precision=lax.Precision.HIGHEST)
    pre = pre + placed.reshape(rows, local_ff)
    hidden = jax.nn.silu(pre).astype(jnp.bfloat16)
    hidden_all = lax.all_gather(hidden, "shard", axis=0, tiled=True)
    partial_out = jnp.dot(hidden_all, w_down, preferred_element_type=jnp.float32)
    partial_out = partial_out.astype(jnp.bfloat16).reshape(shards, lax.axis_size("dp"), -1, w_down.shape[1])
    partial_out = partial_out.transpose(1, 0, 2, 3).reshape(-1, w_down.shape[1])
    out_cols = lax.psum_scatter(partial_out, "dp", scatter_dimension=0, tiled=True)
    layer_out = lax.all_to_all(out_cols, "shard", split_axis=0, concat_axis=1, tiled=True)
    sigma = jax.nn.sigmoid(pre)
    dpre = (back * sigma * (1.0 + pre * (1.0 - sigma))).astype(jnp.bfloat16)
    factor = 1.0 / math.sqrt(rows * shards)
    slope_blocks = dpre.reshape(rows, col_count, side)
    chosen = jnp.einsum(
        "rcb,sc->srb",
        slope_blocks,
        col_onehot.astype(jnp.bfloat16),
        preferred_element_type=jnp.float32,
    ).astype(jnp.bfloat16)
    grads = jnp.einsum("srk,srn->skn", picked, chosen, preferred_element_type=jnp.float32)
    grads = grads * factor
    owned_grad = lax.psum_scatter(
        grads.astype(jnp.bfloat16), "shard", scatter_dimension=0, tiled=True
    ).astype(jnp.float32)
    new_first = 0.9 * first_moment + 0.1 * owned_grad
    new_second = 0.95 * second_moment + 0.05 * owned_grad * owned_grad
    corrected_first = new_first / (1.0 - 0.9**10)
    corrected_second = new_second / (1.0 - 0.95**10)
    new_delta = delta - 0.01 * corrected_first / (jnp.sqrt(corrected_second) + 1e-08)
    return (layer_out, new_delta, new_first, new_second)


def solution(mesh):
    in_specs = (
        P(("dp", "shard"), None),
        P(("dp", "shard"), None),
        P("shard", "dp"),
        P("dp", "shard"),
        P(("dp", "shard"), None, None),
        P(("dp", "shard"), None, None),
        P(("dp", "shard"), None, None),
        P(),
        P(),
        P(),
    )
    out_specs = (
        P(("dp", "shard"), None),
        P(("dp", "shard"), None, None),
        P(("dp", "shard"), None, None),
        P(("dp", "shard"), None, None),
    )
    return jax.shard_map(
        on_device, mesh=mesh, in_specs=in_specs, out_specs=out_specs, check_vma=False
    )
```

```python
import functools
import math

import jax
import jax.numpy as jnp
from jax import lax
from jax.experimental import pallas as pl
from jax.experimental.pallas import tpu as pltpu
from jax.sharding import PartitionSpec as P

F32 = jnp.float32
BF16 = jnp.bfloat16
VMEM_LIMIT = 62 * 1024 * 1024
VMEM_PLAN = 56 * 1024 * 1024


def flip(place, mask):
    bit = 1
    while bit <= mask:
        if mask & bit:
            place = place + bit * (1 - 2 * ((place // bit) % 2))
        bit *= 2
    return place


class Tree:
    def __init__(self, n):
        self.n = n
        self.bits = n.bit_length() - 1
        rest = list(range(1, self.bits))
        self.orders = ([0] + rest, [0] + rest[::-1])

    def first(self, h, j):
        return next(b for b in self.orders[h] if j >> b & 1)

    def children(self, h, j):
        found = []
        for b in self.orders[h]:
            if j >> b & 1:
                break
            found.append(j | 1 << b)
        return found


def tile_of(width):
    tile = min(width, 1024) // 128 * 128
    while width % tile:
        tile -= 128
    return tile


def middle_kernel(
    n, x_ref, d_ref, up_ref, down_ref, placed_ref, out_ref, dpre_ref,
    part, got, hid, pre_s, send_s, recv_s, hsend_s, hrecv_s,
):
    tree = Tree(n)
    me = lax.axis_index("shard")
    rows = placed_ref.shape[0]
    half = part.shape[4]
    tile = tile_of(half)
    tiles = half // tile

    barrier = pltpu.get_barrier_semaphore()
    for b in range(tree.bits):
        pl.semaphore_signal(
            barrier, inc=1, device_id={"shard": flip(me, 1 << b)}, device_id_type=pl.DeviceIdType.MESH
        )
    pl.semaphore_wait(barrier, tree.bits)

    def sum_copy(t, h, j):
        return pltpu.make_async_remote_copy(
            src_ref=part.at[t, h, j],
            dst_ref=got.at[t, h, j],
            send_sem=send_s.at[t, h, j],
            recv_sem=recv_s.at[t, h, j],
            device_id={"shard": flip(me, 1 << tree.first(h, j))},
            device_id_type=pl.DeviceIdType.MESH,
        )

    def hid_copy(h, src, dst):
        return pltpu.make_async_remote_copy(
            src_ref=hid.at[h, src],
            dst_ref=hid.at[h, dst],
            send_sem=hsend_s.at[h, dst],
            recv_sem=hrecv_s.at[h, dst],
            device_id={"shard": flip(me, src ^ dst)},
            device_id_type=pl.DeviceIdType.MESH,
        )

    def chunk(t, h, j):
        source = x_ref if t == 0 else d_ref
        at = pl.ds(pl.multiple_of(flip(me, j) * rows, rows), rows)
        kids = tree.children(h, j)
        for kid in kids:
            sum_copy(t, h, kid).wait_recv()

        def body(i, _):
            cols = pl.ds(pl.multiple_of(i * tile, 128), tile)
            wide = pl.ds(pl.multiple_of(h * half + i * tile, 128), tile)
            if t == 0:
                total = jnp.dot(source[at, :], up_ref[:, wide], preferred_element_type=F32)
            else:
                total = lax.dot_general(
                    source[at, :], down_ref[wide, :], (((1,), (1,)), ((), ())), preferred_element_type=F32
                )
            for kid in kids:
                total = total + got[t, h, kid, :, cols].astype(F32)
            if j:
                part[t, h, j, :, cols] = total.astype(BF16)
            elif t == 0:
                pre = total + placed_ref[:, wide]
                pre_s[h, :, cols] = pre
                hid[h, 0, :, cols] = (pre * jax.nn.sigmoid(pre)).astype(BF16)
            else:
                pre = pre_s[h, :, cols]
                sigma = jax.nn.sigmoid(pre)
                dpre_ref[:, wide] = (total * sigma * (1.0 + pre * (1.0 - sigma))).astype(BF16)
            return 0

        lax.fori_loop(0, tiles, body, 0)
        if j:
            sum_copy(t, h, j).start()

    def project(j):
        at = pl.ds(pl.multiple_of(flip(me, j) * rows, rows), rows)
        total = jnp.dot(hid[0, j], down_ref[pl.ds(0, half), :], preferred_element_type=F32)
        total += jnp.dot(hid[1, j], down_ref[pl.ds(half, half), :], preferred_element_type=F32)
        out_ref[at, :] = total.astype(BF16)

    odd = sorted((j for j in range(n) if j & 1), key=lambda j: -j.bit_count())
    even = [(h, j) for j in range(2, n, 2) for h in range(2)]
    even.sort(key=lambda c: (-c[1].bit_count(), len(tree.children(*c))))
    early = [c for c in even if len(tree.children(*c)) == 1]
    late = [c for c in even if len(tree.children(*c)) > 1]
    for t in range(2):
        for j in odd:
            for h in range(2):
                chunk(t, h, j)
    for h, j in even:
        chunk(0, h, j)
    for h, j in early:
        chunk(1, h, j)
    for h in range(2):
        chunk(0, h, 0)
        for j in sorted(tree.children(h, 0), key=lambda j: -len(tree.children(h, j))):
            hid_copy(h, 0, j).start()
    for h, j in late:
        chunk(1, h, j)
    project(0)
    arrivals = [(h, j) for j in range(1, n) for h in range(2)]
    arrivals.sort(key=lambda c: (c[1].bit_count(), -len(tree.children(*c))))
    seen = [0] * n
    ready = []
    for at, (h, j) in enumerate(arrivals):
        hid_copy(h, j ^ (1 << tree.first(h, j)), j).wait_recv()
        for kid in sorted(tree.children(h, j), key=lambda k: -len(tree.children(h, k))):
            hid_copy(h, j, kid).start()
        seen[j] += 1
        if seen[j] == 2:
            ready.append(j)
        if at + 1 == len(arrivals) or arrivals[at + 1][1].bit_count() > j.bit_count():
            for k in ready:
                project(k)
            ready = []
            if j.bit_count() == 1:
                for k in range(2):
                    chunk(1, k, 0)
    for h in range(2):
        for j in range(1, n):
            for t in range(2):
                sum_copy(t, h, j).wait_send()
            hid_copy(h, j ^ (1 << tree.first(h, j)), j).wait_send()


def middle(n, call, x_cols, d_cols, w_up, w_down, placed):
    rows, wide = placed.shape
    half = wide // 2
    depth = w_down.shape[1]
    vmem = pl.BlockSpec(memory_space=pltpu.VMEM)
    return pl.pallas_call(
        functools.partial(middle_kernel, n),
        out_shape=(
            jax.ShapeDtypeStruct((n * rows, depth), BF16),
            jax.ShapeDtypeStruct((rows, wide), BF16),
        ),
        in_specs=[vmem] * 5,
        out_specs=(vmem, vmem),
        scratch_shapes=[
            pltpu.VMEM((2, 2, n, rows, half), BF16),
            pltpu.VMEM((2, 2, n, rows, half), BF16),
            pltpu.VMEM((2, n, rows, half), BF16),
            pltpu.VMEM((2, rows, half), F32),
            pltpu.SemaphoreType.DMA((2, 2, n)),
            pltpu.SemaphoreType.DMA((2, 2, n)),
            pltpu.SemaphoreType.DMA((2, n)),
            pltpu.SemaphoreType.DMA((2, n)),
        ],
        compiler_params=pltpu.CompilerParams(
            collective_id=call, has_side_effects=True, vmem_limit_bytes=VMEM_LIMIT
        ),
        cost_estimate=pl.CostEstimate(
            flops=6 * n * rows * wide * depth, bytes_accessed=4 * wide * depth, transcendentals=2 * rows * wide
        ),
        name="middle",
    )(x_cols, d_cols, w_up, w_down, placed)


def passes_of(n, rows, wide, depth):
    count = 1
    while True:
        r = rows // count
        need = 10 * n * r * wide * 2 // 2 + 4 * wide * depth + 4 * n * r * depth + 12 * r * wide + 2 * n * r * depth
        if need <= VMEM_PLAN or r % 32:
            return count
        count *= 2


def on_device(
    tokens, cotangent, w_up, w_down, delta, first_moment, second_moment, blk_row, blk_col, live
):
    shards = lax.axis_size("shard")
    own_slots = delta.shape[0]
    side = delta.shape[1]
    gathered_x, gathered_d = (
        lax.all_gather(tokens, "dp", axis=0, tiled=True),
        lax.all_gather(cotangent, "dp", axis=0, tiled=True),
    )
    rows = gathered_x.shape[0]
    width = gathered_x.shape[1]
    local_ff = w_up.shape[1]
    col_count = local_ff // side
    row_count = width // side
    group_index = lax.axis_index("dp")
    group_size = shards * own_slots
    begin = group_index * group_size
    slot_row = lax.dynamic_slice_in_dim(blk_row, begin, group_size)
    slot_col = lax.dynamic_slice_in_dim(blk_col, begin, group_size) - group_index * col_count
    slot_live = lax.dynamic_slice_in_dim(live, begin, group_size).astype(jnp.float32)
    row_onehot = (slot_row[:, None] == jnp.arange(row_count)[None, :]).astype(jnp.float32)
    col_onehot = (slot_col[:, None] == jnp.arange(col_count)[None, :]).astype(
        jnp.float32
    ) * slot_live[:, None]
    blocks = lax.all_gather(delta.astype(jnp.bfloat16), "shard", axis=0, tiled=True)
    x_cols = lax.all_to_all(gathered_x, "shard", split_axis=1, concat_axis=0, tiled=True)
    d_cols = lax.all_to_all(gathered_d, "shard", split_axis=1, concat_axis=0, tiled=True)
    x_blocks = gathered_x.reshape(rows, row_count, side)
    picked = jnp.einsum(
        "rkb,sk->srb", x_blocks, row_onehot.astype(jnp.bfloat16), preferred_element_type=jnp.float32
    ).astype(jnp.bfloat16)
    contrib = jnp.einsum("srb,sbn->srn", picked, blocks, preferred_element_type=jnp.float32)
    placed = jnp.einsum("srn,sc->rcn", contrib, col_onehot, precision=lax.Precision.HIGHEST)
    placed = placed.reshape(rows, local_ff)
    passes = passes_of(shards, rows, local_ff, w_down.shape[1])
    piece = rows // passes
    x_cols = x_cols.reshape(shards, passes, piece, -1)
    d_cols = d_cols.reshape(shards, passes, piece, -1)
    outs, slopes = [], []
    for p in range(passes):
        out, slope = middle(
            shards,
            p,
            x_cols[:, p].reshape(shards * piece, -1),
            d_cols[:, p].reshape(shards * piece, -1),
            w_up,
            w_down,
            placed[p * piece : (p + 1) * piece],
        )
        outs.append(out.reshape(shards, piece, -1))
        slopes.append(slope)
    partial_out = jnp.concatenate(outs, axis=1)
    dpre = jnp.concatenate(slopes, axis=0)
    partial_out = partial_out.reshape(shards, lax.axis_size("dp"), -1, w_down.shape[1])
    partial_out = partial_out.transpose(1, 0, 2, 3).reshape(-1, w_down.shape[1])
    out_cols = lax.psum_scatter(partial_out, "dp", scatter_dimension=0, tiled=True)
    layer_out = lax.all_to_all(out_cols, "shard", split_axis=0, concat_axis=1, tiled=True)
    factor = 1.0 / math.sqrt(rows * shards)
    slope_blocks = dpre.reshape(rows, col_count, side)
    chosen = jnp.einsum(
        "rcb,sc->srb",
        slope_blocks,
        col_onehot.astype(jnp.bfloat16),
        preferred_element_type=jnp.float32,
    ).astype(jnp.bfloat16)
    grads = jnp.einsum("srk,srn->skn", picked, chosen, preferred_element_type=jnp.float32)
    grads = grads * factor
    owned_grad = lax.psum_scatter(
        grads.astype(jnp.bfloat16), "shard", scatter_dimension=0, tiled=True
    ).astype(jnp.float32)
    new_first = 0.9 * first_moment + 0.1 * owned_grad
    new_second = 0.95 * second_moment + 0.05 * owned_grad * owned_grad
    corrected_first = new_first / (1.0 - 0.9**10)
    corrected_second = new_second / (1.0 - 0.95**10)
    new_delta = delta - 0.01 * corrected_first / (jnp.sqrt(corrected_second) + 1e-08)
    return (layer_out, new_delta, new_first, new_second)


def solution(mesh):
    in_specs = (
        P(("dp", "shard"), None),
        P(("dp", "shard"), None),
        P("shard", "dp"),
        P("dp", "shard"),
        P(("dp", "shard"), None, None),
        P(("dp", "shard"), None, None),
        P(("dp", "shard"), None, None),
        P(),
        P(),
        P(),
    )
    out_specs = (
        P(("dp", "shard"), None),
        P(("dp", "shard"), None, None),
        P(("dp", "shard"), None, None),
        P(("dp", "shard"), None, None),
    )
    return jax.shard_map(
        on_device, mesh=mesh, in_specs=in_specs, out_specs=out_specs, check_vma=False
    )
```

```python
import functools
import math

import jax
import jax.numpy as jnp
from jax import lax
from jax.experimental import pallas as pl
from jax.experimental.pallas import tpu as pltpu
from jax.sharding import PartitionSpec as P

F32 = jnp.float32
BF16 = jnp.bfloat16
VMEM_LIMIT = 62 * 1024 * 1024
VMEM_PLAN = 56 * 1024 * 1024


def flip(place, mask):
    bit = 1
    while bit <= mask:
        if mask & bit:
            place = place + bit * (1 - 2 * ((place // bit) % 2))
        bit *= 2
    return place


class Tree:
    def __init__(self, n):
        self.n = n
        self.bits = n.bit_length() - 1
        rest = list(range(1, self.bits))
        self.orders = ([0] + rest, [0] + rest[::-1])

    def first(self, h, j):
        return next(b for b in self.orders[h] if j >> b & 1)

    def children(self, h, j):
        found = []
        for b in self.orders[h]:
            if j >> b & 1:
                break
            found.append(j | 1 << b)
        return found


def tile_of(width):
    tile = min(width, 1024) // 128 * 128
    while width % tile:
        tile -= 128
    return tile


def meet(n, groups, me, group):
    barrier = pltpu.get_barrier_semaphore()
    for j in range(1, n):
        pl.semaphore_signal(
            barrier, inc=1, device_id={"shard": flip(me, j)}, device_id_type=pl.DeviceIdType.MESH
        )
    for k in range(1, groups):
        pl.semaphore_signal(
            barrier, inc=1, device_id={"dp": (group + k) % groups}, device_id_type=pl.DeviceIdType.MESH
        )
    pl.semaphore_wait(barrier, n - 1 + groups - 1)


def group_copies(source, target, groups, group, send_s, recv_s):
    return [
        pltpu.make_async_remote_copy(
            src_ref=source,
            dst_ref=target(),
            send_sem=send_s.at[k],
            recv_sem=recv_s.at[k],
            device_id={"dp": (group + k) % groups},
            device_id_type=pl.DeviceIdType.MESH,
        )
        for k in range(1, groups)
    ]


def front_kernel(
    n, tok_ref, blk_ref, rows_ref, cols_ref, all_ref, zsend_s, zrecv_s, send_s, recv_s, bsend_s, brecv_s
):
    me = lax.axis_index("shard")
    group = lax.axis_index("dp")
    groups = rows_ref.shape[0]
    depth = cols_ref.shape[3]
    meet(n, groups, me, group)
    z_copies = group_copies(tok_ref, lambda: rows_ref.at[group], groups, group, zsend_s, zrecv_s)
    for copy in z_copies:
        copy.start()

    def blk_copy(j):
        return pltpu.make_async_remote_copy(
            src_ref=blk_ref,
            dst_ref=all_ref.at[me],
            send_sem=bsend_s.at[j],
            recv_sem=brecv_s.at[j],
            device_id={"shard": flip(me, j)},
            device_id_type=pl.DeviceIdType.MESH,
        )

    def col_copy(j):
        there = flip(me, j)
        return pltpu.make_async_remote_copy(
            src_ref=rows_ref.at[:, :, pl.ds(pl.multiple_of(there * depth, 128), depth)],
            dst_ref=cols_ref.at[me],
            send_sem=send_s.at[j],
            recv_sem=recv_s.at[j],
            device_id={"shard": there},
            device_id_type=pl.DeviceIdType.MESH,
        )

    for j in range(1, n):
        blk_copy(j).start()
    rows_ref[group] = tok_ref[...]
    all_ref[me] = blk_ref[...]
    for copy in z_copies:
        copy.wait_recv()
    for j in range(n - 1, 0, -1):
        col_copy(j).start()
    cols_ref[me] = rows_ref[:, :, pl.ds(pl.multiple_of(me * depth, 128), depth)]
    for j in range(1, n):
        blk_copy(j).wait()
        col_copy(j).wait()
    for copy in z_copies:
        copy.wait_send()


def front(n, groups, call, tokens, blocks):
    vmem = pl.BlockSpec(memory_space=pltpu.VMEM)
    rows, width = tokens.shape
    return pl.pallas_call(
        functools.partial(front_kernel, n),
        out_shape=(
            jax.ShapeDtypeStruct((groups, rows, width), BF16),
            jax.ShapeDtypeStruct((n, groups, rows, width // n), BF16),
            jax.ShapeDtypeStruct((n,) + blocks.shape, BF16),
        ),
        in_specs=[vmem] * 2,
        out_specs=(vmem,) * 3,
        scratch_shapes=[pltpu.SemaphoreType.DMA((groups,))] * 2 + [pltpu.SemaphoreType.DMA((n,))] * 4,
        compiler_params=pltpu.CompilerParams(
            collective_id=call, has_side_effects=True, vmem_limit_bytes=VMEM_LIMIT // 2
        ),
        name="front",
    )(tokens, blocks)


def back_kernel(
    n, part_ref, grad_ref, out_ref, sum_ref, zgot, ggot, mine, fin,
    zsend_s, zrecv_s, gsend_s, grecv_s, send_s, recv_s,
):
    me = lax.axis_index("shard")
    group = lax.axis_index("dp")
    groups = part_ref.shape[0]
    depth = part_ref.shape[3]
    meet(n, groups, me, group)

    def z_copy(k):
        there = (group + k) % groups
        return pltpu.make_async_remote_copy(
            src_ref=part_ref.at[there],
            dst_ref=zgot.at[k],
            send_sem=zsend_s.at[k],
            recv_sem=zrecv_s.at[k],
            device_id={"dp": there},
            device_id_type=pl.DeviceIdType.MESH,
        )

    def grad_copy(j):
        there = flip(me, j)
        return pltpu.make_async_remote_copy(
            src_ref=grad_ref.at[there],
            dst_ref=ggot.at[j],
            send_sem=gsend_s.at[j],
            recv_sem=grecv_s.at[j],
            device_id={"shard": there},
            device_id_type=pl.DeviceIdType.MESH,
        )

    def out_copy(j):
        return pltpu.make_async_remote_copy(
            src_ref=mine.at[flip(me, j)],
            dst_ref=fin.at[me],
            send_sem=send_s.at[j],
            recv_sem=recv_s.at[j],
            device_id={"shard": flip(me, j)},
            device_id_type=pl.DeviceIdType.MESH,
        )

    for k in range(1, groups):
        z_copy(k).start()
    for j in range(n - 1, 0, -1):
        grad_copy(j).start()
    total = grad_ref[me].astype(F32)
    for j in range(1, n):
        grad_copy(j).wait_recv()
        total += ggot[j].astype(F32)
    sum_ref[...] = total
    total = part_ref[group].astype(F32)
    for k in range(1, groups):
        z_copy(k).wait_recv()
        total += zgot[k].astype(F32)
    mine[...] = total.astype(BF16)
    for j in range(n - 1, 0, -1):
        out_copy(j).start()
    fin[me] = mine[me]
    for j in range(1, n):
        out_copy(j).wait()
        grad_copy(j).wait_send()
    for k in range(1, groups):
        z_copy(k).wait_send()
    for s in range(n):
        out_ref[:, pl.ds(s * depth, depth)] = fin[s]


def back(n, groups, call, part, grads):
    vmem = pl.BlockSpec(memory_space=pltpu.VMEM)
    _, _, rows, depth = part.shape
    return pl.pallas_call(
        functools.partial(back_kernel, n),
        out_shape=(
            jax.ShapeDtypeStruct((rows, n * depth), BF16),
            jax.ShapeDtypeStruct(grads.shape[1:], F32),
        ),
        in_specs=[vmem] * 2,
        out_specs=(vmem,) * 2,
        scratch_shapes=[
            pltpu.VMEM((groups, n, rows, depth), BF16),
            pltpu.VMEM(grads.shape, BF16),
            pltpu.VMEM((n, rows, depth), BF16),
            pltpu.VMEM((n, rows, depth), BF16),
        ]
        + [pltpu.SemaphoreType.DMA((groups,))] * 2
        + [pltpu.SemaphoreType.DMA((n,))] * 4,
        compiler_params=pltpu.CompilerParams(
            collective_id=call, has_side_effects=True, vmem_limit_bytes=VMEM_LIMIT // 2
        ),
        name="back",
    )(part, grads)


def middle_kernel(
    n, x_ref, cot_ref, up_ref, down_ref, placed_ref, out_ref, dpre_ref,
    part, got, hid, pre_s, cot_all, cot_cols,
    send_s, recv_s, hsend_s, hrecv_s, zsend_s, zrecv_s, csend_s, crecv_s,
):
    tree = Tree(n)
    me = lax.axis_index("shard")
    rows = placed_ref.shape[0]
    half = part.shape[4]
    tile = tile_of(half)
    tiles = half // tile

    groups = cot_all.shape[0]
    depth = down_ref.shape[1]
    group = lax.axis_index("dp")
    meet(n, groups, me, group)

    def sum_copy(t, h, j):
        return pltpu.make_async_remote_copy(
            src_ref=part.at[t, h, j],
            dst_ref=got.at[t, h, j],
            send_sem=send_s.at[t, h, j],
            recv_sem=recv_s.at[t, h, j],
            device_id={"shard": flip(me, 1 << tree.first(h, j))},
            device_id_type=pl.DeviceIdType.MESH,
        )

    def cot_copy(j):
        there = flip(me, j)
        return pltpu.make_async_remote_copy(
            src_ref=cot_all.at[:, :, pl.ds(pl.multiple_of(there * depth, 128), depth)],
            dst_ref=cot_cols.at[j],
            send_sem=csend_s.at[j],
            recv_sem=crecv_s.at[j],
            device_id={"shard": there},
            device_id_type=pl.DeviceIdType.MESH,
        )

    def hid_copy(h, src, dst):
        return pltpu.make_async_remote_copy(
            src_ref=hid.at[h, src],
            dst_ref=hid.at[h, dst],
            send_sem=hsend_s.at[h, dst],
            recv_sem=hrecv_s.at[h, dst],
            device_id={"shard": flip(me, src ^ dst)},
            device_id_type=pl.DeviceIdType.MESH,
        )

    landed = set()

    def chunk(t, h, j):
        at = pl.ds(pl.multiple_of(flip(me, j) * rows, rows), rows)
        kids = tree.children(h, j)
        for kid in kids:
            sum_copy(t, h, kid).wait_recv()
        if t == 1 and j and j not in landed:
            landed.add(j)
            cot_copy(j).wait_recv()

        def body(i, _):
            cols = pl.ds(pl.multiple_of(i * tile, 128), tile)
            wide = pl.ds(pl.multiple_of(h * half + i * tile, 128), tile)
            if t == 0:
                total = jnp.dot(x_ref[at, :], up_ref[:, wide], preferred_element_type=F32)
            else:
                total = lax.dot_general(
                    cot_cols[j].reshape(rows, depth),
                    down_ref[wide, :],
                    (((1,), (1,)), ((), ())),
                    preferred_element_type=F32,
                )
            for kid in kids:
                total = total + got[t, h, kid, :, cols].astype(F32)
            if j:
                part[t, h, j, :, cols] = total.astype(BF16)
            elif t == 0:
                pre = total + placed_ref[:, wide]
                pre_s[h, :, cols] = pre
                hid[h, 0, :, cols] = (pre * jax.nn.sigmoid(pre)).astype(BF16)
            else:
                pre = pre_s[h, :, cols]
                sigma = jax.nn.sigmoid(pre)
                dpre_ref[:, wide] = (total * sigma * (1.0 + pre * (1.0 - sigma))).astype(BF16)
            return 0

        lax.fori_loop(0, tiles, body, 0)
        if j:
            sum_copy(t, h, j).start()

    def project(j):
        at = pl.ds(pl.multiple_of(flip(me, j) * rows, rows), rows)
        total = jnp.dot(hid[0, j], down_ref[pl.ds(0, half), :], preferred_element_type=F32)
        total += jnp.dot(hid[1, j], down_ref[pl.ds(half, half), :], preferred_element_type=F32)
        out_ref[at, :] = total.astype(BF16)

    odd = sorted((j for j in range(n) if j & 1), key=lambda j: -j.bit_count())
    even = [(h, j) for j in range(2, n, 2) for h in range(2)]
    even.sort(key=lambda c: (-c[1].bit_count(), len(tree.children(*c))))
    early = [c for c in even if len(tree.children(*c)) == 1]
    late = [c for c in even if len(tree.children(*c)) > 1]
    cot_all[group] = cot_ref[...]
    z_copies = group_copies(cot_ref, lambda: cot_all.at[group], groups, group, zsend_s, zrecv_s)
    for copy in z_copies:
        copy.start()
    for j in odd:
        for h in range(2):
            chunk(0, h, j)
    for h, j in even:
        chunk(0, h, j)
    for copy in z_copies:
        copy.wait_recv()
    for j in odd + sorted({j for _, j in even}, key=lambda j: -j.bit_count()):
        cot_copy(j).start()
    cot_cols[0] = cot_all[:, :, pl.ds(pl.multiple_of(me * depth, 128), depth)]
    for h in range(2):
        chunk(0, h, 0)
        for j in sorted(tree.children(h, 0), key=lambda j: -len(tree.children(h, j))):
            hid_copy(h, 0, j).start()
    for j in odd:
        for h in range(2):
            chunk(1, h, j)
    for h, j in early:
        chunk(1, h, j)
    project(0)
    arrivals = [(h, j) for j in range(1, n) for h in range(2)]
    arrivals.sort(key=lambda c: (c[1].bit_count(), -len(tree.children(*c))))
    for level in range(1, tree.bits + 1):
        now = [c for c in arrivals if c[1].bit_count() == level]
        for h, j in now:
            hid_copy(h, j ^ (1 << tree.first(h, j)), j).wait_recv()
            for kid in sorted(tree.children(h, j), key=lambda k: -len(tree.children(h, k))):
                hid_copy(h, j, kid).start()
        if level == 1:
            for h, j in late:
                chunk(1, h, j)
        if level == min(2, tree.bits):
            for h in range(2):
                chunk(1, h, 0)
        for j in sorted({j for _, j in now}):
            project(j)
    for copy in z_copies:
        copy.wait_send()
    for j in range(1, n):
        cot_copy(j).wait_send()
    for h in range(2):
        for j in range(1, n):
            for t in range(2):
                sum_copy(t, h, j).wait_send()
            hid_copy(h, j ^ (1 << tree.first(h, j)), j).wait_send()


def middle(n, groups, call, x_cols, cotangent, w_up, w_down, placed):
    rows, wide = placed.shape
    half = wide // 2
    depth = w_down.shape[1]
    vmem = pl.BlockSpec(memory_space=pltpu.VMEM)
    return pl.pallas_call(
        functools.partial(middle_kernel, n),
        out_shape=(
            jax.ShapeDtypeStruct((n * rows, depth), BF16),
            jax.ShapeDtypeStruct((rows, wide), BF16),
        ),
        in_specs=[vmem] * 5,
        out_specs=(vmem, vmem),
        scratch_shapes=[
            pltpu.VMEM((2, 2, n, rows, half), BF16),
            pltpu.VMEM((2, 2, n, rows, half), BF16),
            pltpu.VMEM((2, n, rows, half), BF16),
            pltpu.VMEM((2, rows, half), F32),
            pltpu.VMEM((groups,) + cotangent.shape, BF16),
            pltpu.VMEM((n, groups, cotangent.shape[0], depth), BF16),
            pltpu.SemaphoreType.DMA((2, 2, n)),
            pltpu.SemaphoreType.DMA((2, 2, n)),
            pltpu.SemaphoreType.DMA((2, n)),
            pltpu.SemaphoreType.DMA((2, n)),
            pltpu.SemaphoreType.DMA((groups,)),
            pltpu.SemaphoreType.DMA((groups,)),
            pltpu.SemaphoreType.DMA((n,)),
            pltpu.SemaphoreType.DMA((n,)),
        ],
        compiler_params=pltpu.CompilerParams(
            collective_id=call, has_side_effects=True, vmem_limit_bytes=VMEM_LIMIT
        ),
        cost_estimate=pl.CostEstimate(
            flops=6 * n * rows * wide * depth, bytes_accessed=4 * wide * depth, transcendentals=2 * rows * wide
        ),
        name="middle",
    )(x_cols, cotangent, w_up, w_down, placed)


def passes_of(n, rows, wide, depth):
    count = 1
    while True:
        r = rows // count
        need = 10 * n * r * wide * 2 // 2 + 4 * wide * depth + 8 * n * r * depth + 12 * r * wide + 2 * n * r * depth
        if need <= VMEM_PLAN or r % 32:
            return count
        count *= 2


def on_device(
    tokens, cotangent, w_up, w_down, delta, first_moment, second_moment, blk_row, blk_col, live
):
    shards = lax.axis_size("shard")
    own_slots = delta.shape[0]
    side = delta.shape[1]
    groups = lax.axis_size("dp")
    gathered_x, x_cols, blocks = front(shards, groups, 0, tokens, delta.astype(BF16))
    gathered_x = gathered_x.reshape(-1, tokens.shape[1])
    blocks = blocks.reshape(-1, side, side)
    rows = gathered_x.shape[0]
    width = gathered_x.shape[1]
    local_ff = w_up.shape[1]
    col_count = local_ff // side
    row_count = width // side
    group_index = lax.axis_index("dp")
    group_size = shards * own_slots
    begin = group_index * group_size
    slot_row = lax.dynamic_slice_in_dim(blk_row, begin, group_size)
    slot_col = lax.dynamic_slice_in_dim(blk_col, begin, group_size) - group_index * col_count
    slot_live = lax.dynamic_slice_in_dim(live, begin, group_size).astype(jnp.float32)
    row_onehot = (slot_row[:, None] == jnp.arange(row_count)[None, :]).astype(jnp.float32)
    col_onehot = (slot_col[:, None] == jnp.arange(col_count)[None, :]).astype(
        jnp.float32
    ) * slot_live[:, None]
    x_blocks = gathered_x.reshape(rows, row_count, side)
    picked = jnp.einsum(
        "rkb,sk->srb", x_blocks, row_onehot.astype(jnp.bfloat16), preferred_element_type=jnp.float32
    ).astype(jnp.bfloat16)
    contrib = jnp.einsum("srb,sbn->srn", picked, blocks, preferred_element_type=jnp.float32)
    placed = jnp.einsum("srn,sc->rcn", contrib, col_onehot, precision=lax.Precision.HIGHEST)
    placed = placed.reshape(rows, local_ff)
    passes = passes_of(shards, rows, local_ff, w_down.shape[1])
    piece = tokens.shape[0] // passes
    depth = w_down.shape[1]
    x_cols = x_cols.reshape(shards, groups, passes, piece, depth)
    placed = placed.reshape(groups, passes, piece, local_ff)
    outs, slopes = [], []
    for p in range(passes):
        out, slope = middle(
            shards,
            groups,
            2 + p,
            x_cols[:, :, p].reshape(-1, depth),
            cotangent[p * piece : (p + 1) * piece],
            w_up,
            w_down,
            placed[:, p].reshape(-1, local_ff),
        )
        outs.append(out.reshape(shards, groups, piece, depth))
        slopes.append(slope.reshape(groups, piece, local_ff))
    partial_out = jnp.concatenate(outs, axis=2).transpose(1, 0, 2, 3)
    dpre = jnp.concatenate(slopes, axis=1)
    factor = 1.0 / math.sqrt(rows * shards)
    slope_blocks = dpre.reshape(rows, col_count, side)
    chosen = jnp.einsum(
        "rcb,sc->srb",
        slope_blocks,
        col_onehot.astype(jnp.bfloat16),
        preferred_element_type=jnp.float32,
    ).astype(jnp.bfloat16)
    grads = jnp.einsum("srk,srn->skn", picked, chosen, preferred_element_type=jnp.float32)
    grads = grads * factor
    grads = grads.astype(BF16).reshape((shards,) + delta.shape)
    layer_out, owned_grad = back(shards, groups, 1, partial_out, grads)
    new_first = 0.9 * first_moment + 0.1 * owned_grad
    new_second = 0.95 * second_moment + 0.05 * owned_grad * owned_grad
    corrected_first = new_first / (1.0 - 0.9**10)
    corrected_second = new_second / (1.0 - 0.95**10)
    new_delta = delta - 0.01 * corrected_first / (jnp.sqrt(corrected_second) + 1e-08)
    return (layer_out, new_delta, new_first, new_second)


def solution(mesh):
    in_specs = (
        P(("dp", "shard"), None),
        P(("dp", "shard"), None),
        P("shard", "dp"),
        P("dp", "shard"),
        P(("dp", "shard"), None, None),
        P(("dp", "shard"), None, None),
        P(("dp", "shard"), None, None),
        P(),
        P(),
        P(),
    )
    out_specs = (
        P(("dp", "shard"), None),
        P(("dp", "shard"), None, None),
        P(("dp", "shard"), None, None),
        P(("dp", "shard"), None, None),
    )
    return jax.shard_map(
        on_device, mesh=mesh, in_specs=in_specs, out_specs=out_specs, check_vma=False
    )
```

```python
import functools
import math

import jax
import jax.numpy as jnp
from jax import lax
from jax.experimental import pallas as pl
from jax.experimental.pallas import tpu as pltpu
from jax.sharding import PartitionSpec as P

F32 = jnp.float32
BF16 = jnp.bfloat16
VMEM_LIMIT = 62 * 1024 * 1024
VMEM_PLAN = 56 * 1024 * 1024


def flip(place, mask):
    bit = 1
    while bit <= mask:
        if mask & bit:
            place = place + bit * (1 - 2 * ((place // bit) % 2))
        bit *= 2
    return place


class Tree:
    def __init__(self, n):
        self.n = n
        self.bits = n.bit_length() - 1
        rest = list(range(1, self.bits))
        self.orders = ([0] + rest, [0] + rest[::-1])

    def first(self, h, j):
        return next(b for b in self.orders[h] if j >> b & 1)

    def children(self, h, j):
        found = []
        for b in self.orders[h]:
            if j >> b & 1:
                break
            found.append(j | 1 << b)
        return found


def tile_of(width):
    tile = min(width, 1024) // 128 * 128
    while width % tile:
        tile -= 128
    return tile


def meet(n, groups, me, group):
    barrier = pltpu.get_barrier_semaphore()
    for j in range(1, n):
        pl.semaphore_signal(
            barrier, inc=1, device_id={"shard": flip(me, j)}, device_id_type=pl.DeviceIdType.MESH
        )
    for k in range(1, groups):
        pl.semaphore_signal(
            barrier, inc=1, device_id={"dp": (group + k) % groups}, device_id_type=pl.DeviceIdType.MESH
        )
    pl.semaphore_wait(barrier, n - 1 + groups - 1)


def group_copies(source, target, groups, group, send_s, recv_s):
    return [
        pltpu.make_async_remote_copy(
            src_ref=source,
            dst_ref=target(),
            send_sem=send_s.at[k],
            recv_sem=recv_s.at[k],
            device_id={"dp": (group + k) % groups},
            device_id_type=pl.DeviceIdType.MESH,
        )
        for k in range(1, groups)
    ]


def front_kernel(
    n, tok_ref, blk_ref, rows_ref, cols_ref, all_ref, zsend_s, zrecv_s, send_s, recv_s, bsend_s, brecv_s
):
    me = lax.axis_index("shard")
    group = lax.axis_index("dp")
    groups = rows_ref.shape[0]
    depth = cols_ref.shape[3]
    meet(n, groups, me, group)
    z_copies = group_copies(tok_ref, lambda: rows_ref.at[group], groups, group, zsend_s, zrecv_s)
    for copy in z_copies:
        copy.start()

    def blk_copy(j):
        return pltpu.make_async_remote_copy(
            src_ref=blk_ref,
            dst_ref=all_ref.at[me],
            send_sem=bsend_s.at[j],
            recv_sem=brecv_s.at[j],
            device_id={"shard": flip(me, j)},
            device_id_type=pl.DeviceIdType.MESH,
        )

    def col_copy(k, j):
        there = flip(me, j)
        source = (group + groups - k) % groups
        return pltpu.make_async_remote_copy(
            src_ref=rows_ref.at[source, :, pl.ds(pl.multiple_of(there * depth, 128), depth)],
            dst_ref=cols_ref.at[me, source],
            send_sem=send_s.at[k, j],
            recv_sem=recv_s.at[k, j],
            device_id={"shard": there},
            device_id_type=pl.DeviceIdType.MESH,
        )

    for j in range(1, n):
        blk_copy(j).start()
    rows_ref[group] = tok_ref[...]
    all_ref[me] = blk_ref[...]
    for k in range(groups):
        if k:
            z_copies[k - 1].wait_recv()
        for j in range(n - 1, 0, -1):
            col_copy(k, j).start()
    cols_ref[me] = rows_ref[:, :, pl.ds(pl.multiple_of(me * depth, 128), depth)]
    for j in range(1, n):
        blk_copy(j).wait()
        for k in range(groups):
            col_copy(k, j).wait()
    for copy in z_copies:
        copy.wait_send()


def front(n, groups, call, tokens, blocks):
    vmem = pl.BlockSpec(memory_space=pltpu.VMEM)
    rows, width = tokens.shape
    return pl.pallas_call(
        functools.partial(front_kernel, n),
        out_shape=(
            jax.ShapeDtypeStruct((groups, rows, width), BF16),
            jax.ShapeDtypeStruct((n, groups, rows, width // n), BF16),
            jax.ShapeDtypeStruct((n,) + blocks.shape, BF16),
        ),
        in_specs=[vmem] * 2,
        out_specs=(vmem,) * 3,
        scratch_shapes=[pltpu.SemaphoreType.DMA((groups,))] * 2
        + [pltpu.SemaphoreType.DMA((groups, n))] * 2
        + [pltpu.SemaphoreType.DMA((n,))] * 2,
        compiler_params=pltpu.CompilerParams(
            collective_id=call, has_side_effects=True, vmem_limit_bytes=VMEM_LIMIT // 2
        ),
        name="front",
    )(tokens, blocks)


def back_kernel(
    n, groups, mine_ref, grad_ref, out_ref, sum_ref, ggot, fin, gsend_s, grecv_s, send_s, recv_s
):
    me = lax.axis_index("shard")
    group = lax.axis_index("dp")
    depth = mine_ref.shape[2]
    meet(n, groups, me, group)

    def grad_copy(j):
        there = flip(me, j)
        return pltpu.make_async_remote_copy(
            src_ref=grad_ref.at[there],
            dst_ref=ggot.at[j],
            send_sem=gsend_s.at[j],
            recv_sem=grecv_s.at[j],
            device_id={"shard": there},
            device_id_type=pl.DeviceIdType.MESH,
        )

    def out_copy(j):
        return pltpu.make_async_remote_copy(
            src_ref=mine_ref.at[flip(me, j)],
            dst_ref=fin.at[me],
            send_sem=send_s.at[j],
            recv_sem=recv_s.at[j],
            device_id={"shard": flip(me, j)},
            device_id_type=pl.DeviceIdType.MESH,
        )

    for j in range(n - 1, 0, -1):
        grad_copy(j).start()
    for j in range(n - 1, 0, -1):
        out_copy(j).start()
    fin[me] = mine_ref[me]
    total = grad_ref[me].astype(F32)
    for j in range(1, n):
        grad_copy(j).wait_recv()
        total += ggot[j].astype(F32)
    sum_ref[...] = total
    for j in range(1, n):
        out_copy(j).wait()
        grad_copy(j).wait_send()
    for s in range(n):
        out_ref[:, pl.ds(s * depth, depth)] = fin[s]


def back(n, groups, call, mine, grads):
    vmem = pl.BlockSpec(memory_space=pltpu.VMEM)
    _, rows, depth = mine.shape
    return pl.pallas_call(
        functools.partial(back_kernel, n, groups),
        out_shape=(
            jax.ShapeDtypeStruct((rows, n * depth), BF16),
            jax.ShapeDtypeStruct(grads.shape[1:], F32),
        ),
        in_specs=[vmem] * 2,
        out_specs=(vmem,) * 2,
        scratch_shapes=[
            pltpu.VMEM(grads.shape, BF16),
            pltpu.VMEM((n, rows, depth), BF16),
        ]
        + [pltpu.SemaphoreType.DMA((n,))] * 4,
        compiler_params=pltpu.CompilerParams(
            collective_id=call, has_side_effects=True, vmem_limit_bytes=VMEM_LIMIT // 2
        ),
        name="back",
    )(mine, grads)


def middle_kernel(
    n, x_ref, cot_ref, up_ref, down_ref, placed_ref, out_ref, dpre_ref,
    part, got, hid, pre_s, cot_all, cot_cols, outs, outs_got,
    send_s, recv_s, hsend_s, hrecv_s, zsend_s, zrecv_s, csend_s, crecv_s, osend_s, orecv_s,
):
    tree = Tree(n)
    me = lax.axis_index("shard")
    rows, lane = placed_ref.shape[1:]
    half = part.shape[4]
    tile = tile_of(half)
    tiles = half // tile

    groups = cot_all.shape[0]
    depth = down_ref.shape[1]
    group = lax.axis_index("dp")
    meet(n, groups, me, group)

    def sum_copy(t, h, j):
        return pltpu.make_async_remote_copy(
            src_ref=part.at[t, h, j],
            dst_ref=got.at[t, h, j],
            send_sem=send_s.at[t, h, j],
            recv_sem=recv_s.at[t, h, j],
            device_id={"shard": flip(me, 1 << tree.first(h, j))},
            device_id_type=pl.DeviceIdType.MESH,
        )

    def cot_copy(j):
        there = flip(me, j)
        return pltpu.make_async_remote_copy(
            src_ref=cot_all.at[:, :, pl.ds(pl.multiple_of(there * depth, 128), depth)],
            dst_ref=cot_cols.at[j],
            send_sem=csend_s.at[j],
            recv_sem=crecv_s.at[j],
            device_id={"shard": there},
            device_id_type=pl.DeviceIdType.MESH,
        )

    def hid_copy(h, src, dst):
        return pltpu.make_async_remote_copy(
            src_ref=hid.at[h, src],
            dst_ref=hid.at[h, dst],
            send_sem=hsend_s.at[h, dst],
            recv_sem=hrecv_s.at[h, dst],
            device_id={"shard": flip(me, src ^ dst)},
            device_id_type=pl.DeviceIdType.MESH,
        )

    landed = set()

    def chunk(t, h, j):
        at = pl.ds(pl.multiple_of(flip(me, j) * rows, rows), rows)
        kids = tree.children(h, j)
        for kid in kids:
            sum_copy(t, h, kid).wait_recv()
        if t == 1 and j and j not in landed:
            landed.add(j)
            cot_copy(j).wait_recv()

        def body(i, _):
            cols = pl.ds(pl.multiple_of(i * tile, 128), tile)
            wide = pl.ds(pl.multiple_of(h * half + i * tile, 128), tile)
            begin = h * (half // lane) + i * (tile // lane)
            if t == 0:
                total = jnp.dot(x_ref[at, :], up_ref[:, wide], preferred_element_type=F32)
            else:
                total = lax.dot_general(
                    cot_cols[j].reshape(rows, depth),
                    down_ref[wide, :],
                    (((1,), (1,)), ((), ())),
                    preferred_element_type=F32,
                )
            for kid in kids:
                total = total + got[t, h, kid, :, cols].astype(F32)
            if j:
                part[t, h, j, :, cols] = total.astype(BF16)
            elif t == 0:
                pre = total + jnp.concatenate([placed_ref[begin + q] for q in range(tile // lane)], axis=1)
                pre_s[h, :, cols] = pre
                hid[h, 0, :, cols] = (pre * jax.nn.sigmoid(pre)).astype(BF16)
            else:
                pre = pre_s[h, :, cols]
                sigma = jax.nn.sigmoid(pre)
                slope = (total * sigma * (1.0 + pre * (1.0 - sigma))).astype(BF16)
                for q in range(tile // lane):
                    dpre_ref[begin + q] = slope[:, q * lane : (q + 1) * lane]
            return 0

        lax.fori_loop(0, tiles, body, 0)
        if j:
            sum_copy(t, h, j).start()

    def out_copy(j, k):
        there = (group + k) % groups
        return pltpu.make_async_remote_copy(
            src_ref=outs.at[j, there],
            dst_ref=outs_got.at[j, k],
            send_sem=osend_s.at[j, k],
            recv_sem=orecv_s.at[j, k],
            device_id={"dp": there},
            device_id_type=pl.DeviceIdType.MESH,
        )

    def project(j):
        total = jnp.dot(hid[0, j], down_ref[pl.ds(0, half), :], preferred_element_type=F32)
        total += jnp.dot(hid[1, j], down_ref[pl.ds(half, half), :], preferred_element_type=F32)
        outs[j] = total.astype(BF16).reshape(outs.shape[1:])
        for k in range(1, groups):
            out_copy(j, k).start()

    odd = sorted((j for j in range(n) if j & 1), key=lambda j: -j.bit_count())
    even = [(h, j) for j in range(2, n, 2) for h in range(2)]
    even.sort(key=lambda c: (-c[1].bit_count(), len(tree.children(*c))))
    early = [c for c in even if len(tree.children(*c)) == 1]
    late = [c for c in even if len(tree.children(*c)) > 1]
    cot_all[group] = cot_ref[...]
    z_copies = group_copies(cot_ref, lambda: cot_all.at[group], groups, group, zsend_s, zrecv_s)
    for copy in z_copies:
        copy.start()
    for j in odd:
        for h in range(2):
            chunk(0, h, j)
    for h, j in even:
        chunk(0, h, j)
    for copy in z_copies:
        copy.wait_recv()
    for j in odd + sorted({j for _, j in even}, key=lambda j: -j.bit_count()):
        cot_copy(j).start()
    cot_cols[0] = cot_all[:, :, pl.ds(pl.multiple_of(me * depth, 128), depth)]
    for h in range(2):
        chunk(0, h, 0)
        for j in sorted(tree.children(h, 0), key=lambda j: -len(tree.children(h, j))):
            hid_copy(h, 0, j).start()
    for j in odd:
        for h in range(2):
            chunk(1, h, j)
    for h, j in early:
        chunk(1, h, j)
    project(0)
    arrivals = [(h, j) for j in range(1, n) for h in range(2)]
    arrivals.sort(key=lambda c: (c[1].bit_count(), -len(tree.children(*c))))
    for level in range(1, tree.bits + 1):
        now = [c for c in arrivals if c[1].bit_count() == level]
        for h, j in now:
            hid_copy(h, j ^ (1 << tree.first(h, j)), j).wait_recv()
            for kid in sorted(tree.children(h, j), key=lambda k: -len(tree.children(h, k))):
                hid_copy(h, j, kid).start()
        if level == 1:
            for h, j in late:
                chunk(1, h, j)
        if level == min(2, tree.bits):
            for h in range(2):
                chunk(1, h, 0)
        for j in sorted({j for _, j in now}):
            project(j)
    for j in sorted(range(n), key=lambda j: j.bit_count()):
        total = outs[j, group].astype(F32)
        for k in range(1, groups):
            out_copy(j, k).wait_recv()
            total += outs_got[j, k].astype(F32)
        out_ref[flip(me, j)] = total.astype(BF16)
    for j in range(n):
        for k in range(1, groups):
            out_copy(j, k).wait_send()
    for copy in z_copies:
        copy.wait_send()
    for j in range(1, n):
        cot_copy(j).wait_send()
    for h in range(2):
        for j in range(1, n):
            for t in range(2):
                sum_copy(t, h, j).wait_send()
            hid_copy(h, j ^ (1 << tree.first(h, j)), j).wait_send()


def middle(n, groups, call, x_cols, cotangent, w_up, w_down, placed):
    chunks, rows, lane = placed.shape
    wide = chunks * lane
    half = wide // 2
    piece = cotangent.shape[0]
    depth = w_down.shape[1]
    vmem = pl.BlockSpec(memory_space=pltpu.VMEM)
    return pl.pallas_call(
        functools.partial(middle_kernel, n),
        out_shape=(
            jax.ShapeDtypeStruct((n, piece, depth), BF16),
            jax.ShapeDtypeStruct(placed.shape, BF16),
        ),
        in_specs=[vmem] * 5,
        out_specs=(vmem, vmem),
        scratch_shapes=[
            pltpu.VMEM((2, 2, n, rows, half), BF16),
            pltpu.VMEM((2, 2, n, rows, half), BF16),
            pltpu.VMEM((2, n, rows, half), BF16),
            pltpu.VMEM((2, rows, half), F32),
            pltpu.VMEM((groups,) + cotangent.shape, BF16),
            pltpu.VMEM((n, groups, piece, depth), BF16),
            pltpu.VMEM((n, groups, piece, depth), BF16),
            pltpu.VMEM((n, groups, piece, depth), BF16),
            pltpu.SemaphoreType.DMA((2, 2, n)),
            pltpu.SemaphoreType.DMA((2, 2, n)),
            pltpu.SemaphoreType.DMA((2, n)),
            pltpu.SemaphoreType.DMA((2, n)),
            pltpu.SemaphoreType.DMA((groups,)),
            pltpu.SemaphoreType.DMA((groups,)),
            pltpu.SemaphoreType.DMA((n,)),
            pltpu.SemaphoreType.DMA((n,)),
            pltpu.SemaphoreType.DMA((n, groups)),
            pltpu.SemaphoreType.DMA((n, groups)),
        ],
        compiler_params=pltpu.CompilerParams(
            collective_id=call, has_side_effects=True, vmem_limit_bytes=VMEM_LIMIT
        ),
        cost_estimate=pl.CostEstimate(
            flops=6 * n * rows * wide * depth, bytes_accessed=4 * wide * depth, transcendentals=2 * rows * wide
        ),
        name="middle",
    )(x_cols, cotangent, w_up, w_down, placed)


def passes_of(n, rows, wide, depth):
    count = 1
    while True:
        r = rows // count
        need = 10 * n * r * wide * 2 // 2 + 4 * wide * depth + 8 * n * r * depth + 12 * r * wide + 2 * n * r * depth
        if need <= VMEM_PLAN or r % 32:
            return count
        count *= 2


def on_device(
    tokens, cotangent, w_up, w_down, delta, first_moment, second_moment, blk_row, blk_col, live
):
    shards = lax.axis_size("shard")
    own_slots = delta.shape[0]
    side = delta.shape[1]
    groups = lax.axis_size("dp")
    gathered_x, x_cols, blocks = front(shards, groups, 0, tokens, delta.astype(BF16))
    gathered_x = gathered_x.reshape(-1, tokens.shape[1])
    blocks = blocks.reshape(-1, side, side)
    rows = gathered_x.shape[0]
    width = gathered_x.shape[1]
    local_ff = w_up.shape[1]
    col_count = local_ff // side
    row_count = width // side
    group_index = lax.axis_index("dp")
    group_size = shards * own_slots
    begin = group_index * group_size
    slot_row = lax.dynamic_slice_in_dim(blk_row, begin, group_size)
    slot_col = lax.dynamic_slice_in_dim(blk_col, begin, group_size) - group_index * col_count
    slot_live = lax.dynamic_slice_in_dim(live, begin, group_size).astype(jnp.float32)
    row_onehot = (slot_row[:, None] == jnp.arange(row_count)[None, :]).astype(jnp.float32)
    col_onehot = (slot_col[:, None] == jnp.arange(col_count)[None, :]).astype(
        jnp.float32
    ) * slot_live[:, None]
    x_blocks = gathered_x.reshape(rows, row_count, side)
    picked = jnp.einsum(
        "rkb,sk->srb", x_blocks, row_onehot.astype(jnp.bfloat16), preferred_element_type=jnp.float32
    ).astype(jnp.bfloat16)
    contrib = jnp.einsum("srb,sbn->srn", picked, blocks, preferred_element_type=jnp.float32)
    placed = jnp.einsum("srn,sc->crn", contrib, col_onehot, precision=lax.Precision.HIGHEST)
    passes = passes_of(shards, rows, local_ff, w_down.shape[1])
    piece = tokens.shape[0] // passes
    depth = w_down.shape[1]
    x_cols = x_cols.reshape(shards, groups, passes, piece, depth)
    placed = placed.reshape(col_count, groups, passes, piece, side)
    outs, slopes = [], []
    for p in range(passes):
        out, slope = middle(
            shards,
            groups,
            2 + p,
            x_cols[:, :, p].reshape(-1, depth),
            cotangent[p * piece : (p + 1) * piece],
            w_up,
            w_down,
            placed[:, :, p].reshape(col_count, -1, side),
        )
        outs.append(out)
        slopes.append(slope.reshape(col_count, groups, piece, side))
    own_out = jnp.concatenate(outs, axis=1)
    slope_blocks = jnp.concatenate(slopes, axis=2).reshape(col_count, rows, side)
    factor = 1.0 / math.sqrt(rows * shards)
    chosen = jnp.einsum(
        "crb,sc->srb",
        slope_blocks,
        col_onehot.astype(jnp.bfloat16),
        preferred_element_type=jnp.float32,
    ).astype(jnp.bfloat16)
    grads = jnp.einsum("srk,srn->skn", picked, chosen, preferred_element_type=jnp.float32)
    grads = grads * factor
    grads = grads.astype(BF16).reshape((shards,) + delta.shape)
    layer_out, owned_grad = back(shards, groups, 1, own_out, grads)
    new_first = 0.9 * first_moment + 0.1 * owned_grad
    new_second = 0.95 * second_moment + 0.05 * owned_grad * owned_grad
    corrected_first = new_first / (1.0 - 0.9**10)
    corrected_second = new_second / (1.0 - 0.95**10)
    new_delta = delta - 0.01 * corrected_first / (jnp.sqrt(corrected_second) + 1e-08)
    return (layer_out, new_delta, new_first, new_second)


def solution(mesh):
    in_specs = (
        P(("dp", "shard"), None),
        P(("dp", "shard"), None),
        P("shard", "dp"),
        P("dp", "shard"),
        P(("dp", "shard"), None, None),
        P(("dp", "shard"), None, None),
        P(("dp", "shard"), None, None),
        P(),
        P(),
        P(),
    )
    out_specs = (
        P(("dp", "shard"), None),
        P(("dp", "shard"), None, None),
        P(("dp", "shard"), None, None),
        P(("dp", "shard"), None, None),
    )
    return jax.shard_map(
        on_device, mesh=mesh, in_specs=in_specs, out_specs=out_specs, check_vma=False
    )
```
